32 devices in a mesh: groups: 2 (over x), row: 8 (over z, y), col: 2 (over core).
Axes of the slice: x: 2, y: 2, z: 4, core: 2. Of those that a mesh axis runs over, the one named last changes fastest.
Arguments:
- features: bfloat16 [8192, 128], P(('groups', 'row', 'col')), parts along dimension 0, may hold values from -6 to 6
- node_order: int32 [32, 256], P(('groups', 'row', 'col')), parts along dimension 0, may hold values from 0 to 255, each once within a row
- weight_first: bfloat16 [128, 256], replicated, may hold values from -0.5 to 0.5
- weight_second: bfloat16 [256, 128], replicated, may hold values from -0.375 to 0.375
- adjacency_tiles: bfloat16 [16, 2, 32, 128, 128], P(('groups', 'row'), 'col'), parts along dimension 0, as said below
- tile_rows: int32 [16, 2, 32], P(('groups', 'row'), 'col'), parts along dimension 0, may hold values from 0 to 3, as said below
- tile_cols: int32 [16, 2, 32], P(('groups', 'row'), 'col'), parts along dimension 0, may hold values from 0 to 15, as said below
- tile_counts: int32 [16, 2], P(('groups', 'row'), 'col'), parts along dimension 0, may hold values from 1 to 32, as said below
- logit_grads: bfloat16 [8192, 128], P(('groups', 'row', 'col')), parts along dimension 0, may hold values from -6 to 6
Outputs:
- logits: bfloat16 [8192, 128], P(('groups', 'row', 'col')), parts along dimension 0
- grad_first: float32 [256, 256], P('groups'), parts along dimension 0
- grad_second: float32 [512, 128], P('groups'), parts along dimension 0
The draws below stay inside these ranges and needn't reach their ends.
There are 2 independent parts, one for each index of `groups`. The reference program is written for one: setup_inputs(seed, part) draws one part's arguments, and reference() takes and returns one part's arrays. A program takes and returns all parts, laid end to end along the dimension named above; an argument that names none is the same for every part. Nothing has to cross between parts.
Inputs may be any that keep to these rules, and one draw needn't show every extreme that they name: `adjacency_tiles`: the live slots of a device name distinct block positions. The adjacency is symmetric: block (j, i) is present exactly when block (i, j) is, and holds its transpose. `tile_rows`: row block of a slot inside its device's row slab. `tile_cols`: column block of a slot inside its device's column set. `tile_counts`: every diagonal block is present. Some device holds exactly 32 live slots in every draw.
All inputs are finite; a program needn't handle non-finite values.
Results may differ from the reference program's by a relative error of at most 0.0055.
Values may be sent and summed in bfloat16 or wider, within the bound.
No kernel may reach another device: no remote copies, remote signals or barrier semaphores. Data moves between devices by JAX's collectives and lax.ppermute only.
A program may use at most 128 MiB of HBM per device.

```python
import math
import jax
import jax.numpy as jnp
from jax import lax

FEAT = 128
HID = 256
CLASSES = 128
BS = 128
BLK_DEV = 2
NODE_DEV = 256
PIECES = 16
NODES = 4096
NBLK = 32
SLAB_BLK = 4
SET_BLK = 16
TILES_DEV = 32
N_ROW = 8
N_COL = 2


def tile_layout(key):
    subkeys = jax.random.split(key, 4)
    shuffled = jax.random.permutation(subkeys[0], NBLK - 1).astype(jnp.int32) + 1
    chosen = jnp.concatenate([jnp.zeros((1,), jnp.int32), shuffled[:NBLK // 2 - 1]])
    in_set = jnp.zeros((NBLK,), jnp.int32).at[chosen].set(1)
    levels = jax.random.randint(subkeys[1], (N_ROW,), 6, 33)
    kept = jax.random.randint(subkeys[2], (), 0, N_ROW * N_COL)
    rolls = jax.random.randint(subkeys[3], (NBLK, NBLK), 0, 1024)
    block_index = jnp.arange(NBLK, dtype=jnp.int32)
    rolls = jnp.where(block_index[:, None] <= block_index[None, :], rolls, rolls.T)
    slab_of = block_index // SLAB_BLK
    owner = slab_of[:, None] * N_COL + block_index[None, :] // BLK_DEV % N_COL
    level_rows = levels[slab_of]
    retained = (rolls < level_rows[:, None] * level_rows[None, :]) | (block_index[:, None] == block_index[None, :]) | (owner == kept) | (owner.T == kept)
    present = (in_set[jnp.bitwise_xor(block_index[:, None], block_index[None, :])] == 1) & retained
    device_row = jnp.arange(N_ROW, dtype=jnp.int32)[:, None, None, None]
    device_col = jnp.arange(N_COL, dtype=jnp.int32)[None, :, None, None]
    local_row = jnp.arange(SLAB_BLK, dtype=jnp.int32)[None, None, :, None]
    local_col = jnp.arange(SET_BLK, dtype=jnp.int32)[None, None, None, :]
    global_row = device_row * SLAB_BLK + local_row
    global_col = (local_col // BLK_DEV * N_COL + device_col) * BLK_DEV + local_col % BLK_DEV
    global_row = jnp.broadcast_to(global_row, (N_ROW, N_COL, SLAB_BLK, SET_BLK))
    global_col = jnp.broadcast_to(global_col, (N_ROW, N_COL, SLAB_BLK, SET_BLK))
    region = present[global_row, global_col]
    flat_region = region.reshape(N_ROW, N_COL, SLAB_BLK * SET_BLK).astype(jnp.int32)
    ranked = jnp.argsort(1 - flat_region, axis=-1, stable=True)[..., :TILES_DEV].astype(jnp.int32)
    live_counts = jnp.sum(flat_region, axis=-1).astype(jnp.int32)
    return (ranked // SET_BLK, ranked % SET_BLK, live_counts)


def draw_tile_rows(key, part):
    return tile_layout(key)[0]


def draw_tile_cols(key, part):
    return tile_layout(key)[1]


def draw_tile_counts(key, part):
    return tile_layout(key)[2]


def draw_adjacency_tiles(key, part):
    local_rows, local_cols, live_counts = tile_layout(key)
    key = jax.random.fold_in(key, 11)
    device_row = jnp.arange(N_ROW, dtype=jnp.int32)[:, None, None]
    device_col = jnp.arange(N_COL, dtype=jnp.int32)[None, :, None]
    global_row = (device_row * SLAB_BLK + local_rows).reshape(-1)
    global_col = ((local_cols // BLK_DEV * N_COL + device_col) * BLK_DEV + local_cols % BLK_DEV).reshape(-1)
    lower_id = jnp.minimum(global_row, global_col)
    upper_id = jnp.maximum(global_row, global_col)
    pair_ids = lower_id * NBLK + upper_id
    same_block = global_row == global_col
    above = global_row < global_col
    spread = 1.0 / math.sqrt(BS * NBLK / 4.0)
    identity_tile = jnp.eye(BS, dtype=jnp.float32)

    def one_tile(inputs):
        pair_id, is_same, is_above = inputs
        matrix = jax.random.normal(jax.random.fold_in(key, pair_id), (BS, BS), jnp.float32)
        mirrored = (matrix + matrix.T) * 0.7071067811865476
        chosen_tile = jnp.where(is_same, mirrored, jnp.where(is_above, matrix, matrix.T))
        return chosen_tile * spread + jnp.where(is_same, 0.5, 0.0) * identity_tile
    values = lax.map(one_tile, (pair_ids, same_block, above))
    return values.reshape(N_ROW, N_COL, TILES_DEV, BS, BS).astype(jnp.bfloat16)


def shard_levels(rng, dims, cuts, low, largest):
    gain, own = 1.0, jax.random.fold_in(rng, 6)
    for position, shards_of in cuts:
        heights = jnp.exp(jax.random.uniform(jax.random.fold_in(own, position), (shards_of,), jnp.float32, low / len(cuts), largest / len(cuts)))
        gain = gain * jnp.repeat(heights, dims[position] // shards_of).reshape([-1 if axis == position else 1 for axis in range(len(dims))])
    return gain


def normal_values(own_key, dims, scale, most, shards=(), kind=jnp.bfloat16):
    gain = shard_levels(own_key, dims, shards, -0.22, 0.18) if shards else 1.0
    drawn = jax.random.normal(own_key, dims, jnp.float32) * scale * gain
    return jnp.minimum(jnp.maximum(drawn, -most), most).astype(kind)


def setup_inputs(seed: int = 0, part: int = 0) -> dict:
    key_list = jax.random.split(jax.random.key(seed), 10)
    part_splits = jax.random.split(jax.random.fold_in(key_list[9], part), 10)
    features = normal_values(part_splits[0], (NODES, FEAT), 1.0, 6.0, ((0, 16),))
    node_order = jax.vmap(lambda own: jax.random.permutation(own, NODE_DEV))(jax.random.split(part_splits[1], PIECES)).reshape((PIECES, NODE_DEV)).astype(jnp.int32)
    weight_first = normal_values(key_list[2], (FEAT, HID), FEAT ** -0.5, 0.5)
    weight_second = normal_values(key_list[3], (HID, CLASSES), HID ** -0.5, 0.375)
    adjacency_tiles = draw_adjacency_tiles(jax.random.fold_in(jax.random.fold_in(key_list[9], part), 71), part)
    tile_rows = draw_tile_rows(jax.random.fold_in(jax.random.fold_in(key_list[9], part), 71), part)
    tile_cols = draw_tile_cols(jax.random.fold_in(jax.random.fold_in(key_list[9], part), 71), part)
    tile_counts = draw_tile_counts(jax.random.fold_in(jax.random.fold_in(key_list[9], part), 71), part)
    logit_grads = normal_values(part_splits[8], (NODES, CLASSES), 1.0, 6.0, ((0, 16),))
    return dict(features=features, node_order=node_order, weight_first=weight_first, weight_second=weight_second, adjacency_tiles=adjacency_tiles, tile_rows=tile_rows, tile_cols=tile_cols, tile_counts=tile_counts, logit_grads=logit_grads)


def aggregate(adjacency_tiles, tile_rows, tile_cols, tile_counts, source_blocks, transposed):
    device_total = N_ROW * N_COL
    tile_flat = adjacency_tiles.reshape(device_total, TILES_DEV, BS, BS)
    rows_flat = tile_rows.reshape(device_total, TILES_DEV)
    cols_flat = tile_cols.reshape(device_total, TILES_DEV)
    counts_flat = tile_counts.reshape(device_total)
    device_ids = jnp.arange(device_total, dtype=jnp.int32)

    def one_device(running, inputs):
        tile_set, local_rows, local_cols, live_count, device_id = inputs
        device_row = device_id // N_COL
        device_col = device_id % N_COL
        global_row = (device_row * SLAB_BLK + local_rows).astype(jnp.int32)
        global_col = ((local_cols // BLK_DEV * N_COL + device_col) * BLK_DEV + local_cols % BLK_DEV).astype(jnp.int32)
        live_mask = jnp.arange(TILES_DEV, dtype=jnp.int32) < live_count
        tile_wide = tile_set.astype(jnp.float32)
        if transposed:
            picked = source_blocks[global_row]
            product = jnp.einsum('tkm,tkf->tmf', tile_wide, picked)
            target = global_col
        else:
            picked = source_blocks[global_col]
            product = jnp.einsum('tmk,tkf->tmf', tile_wide, picked)
            target = global_row
        target = jnp.where(live_mask, target, NBLK).astype(jnp.int32)
        summed = jax.ops.segment_sum(product, target, num_segments=NBLK + 1)[:NBLK]
        return (running + summed, None)
    initial = jnp.zeros((NBLK, BS, source_blocks.shape[-1]), jnp.float32)
    running, _ = lax.scan(one_device, initial, (tile_flat, rows_flat, cols_flat, counts_flat, device_ids))
    return running.reshape(NODES, source_blocks.shape[-1])

def reference(features, node_order, weight_first, weight_second, adjacency_tiles, tile_rows, tile_cols, tile_counts, logit_grads):
    pieces = features.reshape(PIECES, NODE_DEV, FEAT)
    ordered = jnp.take_along_axis(pieces, node_order[:, :, None], axis=1).reshape(NODES, FEAT)
    source_first = ordered.astype(jnp.float32).reshape(NBLK, BS, FEAT)
    aggregated = aggregate(adjacency_tiles, tile_rows, tile_cols, tile_counts, source_first, False).astype(jnp.bfloat16)
    pre_act = jnp.dot(aggregated, weight_first, preferred_element_type=jnp.float32)
    hidden = jax.nn.silu(pre_act).astype(jnp.bfloat16)
    projected = jnp.dot(hidden, weight_second, preferred_element_type=jnp.float32).astype(jnp.bfloat16)
    source_second = projected.astype(jnp.float32).reshape(NBLK, BS, CLASSES)
    logits = aggregate(adjacency_tiles, tile_rows, tile_cols, tile_counts, source_second, False).astype(jnp.bfloat16)
    source_back = logit_grads.astype(jnp.float32).reshape(NBLK, BS, CLASSES)
    back_grads = aggregate(adjacency_tiles, tile_rows, tile_cols, tile_counts, source_back, True).astype(jnp.bfloat16)
    grad_scale = 1.0 / math.sqrt(NODES)
    grad_second = jnp.dot(hidden.T, back_grads, preferred_element_type=jnp.float32) * grad_scale
    hidden_grads = jnp.dot(back_grads, weight_second.T, preferred_element_type=jnp.float32)
    sigmoid_pre = jax.nn.sigmoid(pre_act)
    pre_grads = (hidden_grads * sigmoid_pre * (1.0 + pre_act * (1.0 - sigmoid_pre))).astype(jnp.bfloat16)
    grad_first = jnp.dot(aggregated.T, pre_grads, preferred_element_type=jnp.float32) * grad_scale
    return (logits, grad_first, grad_second)
```

```python
import functools
import math

import jax
import jax.numpy as jnp
from jax import lax
from jax.experimental import pallas as pl
from jax.experimental.pallas import tpu as pltpu
from jax.sharding import PartitionSpec as P

VMEM = pl.BlockSpec(memory_space=pltpu.VMEM)
SMEM = pl.BlockSpec(memory_space=pltpu.SMEM)


def dot(a, b, contract=((1,), (0,))):
    return lax.dot_general(a, b, (contract, ((), ())), preferred_element_type=jnp.float32)


def call(kernel, out_shape, in_specs, flops, name, *args):
    total = sum(a.size * a.dtype.itemsize for a in args)
    outs = out_shape if isinstance(out_shape, (tuple, list)) else (out_shape,)
    total += sum(math.prod(o.shape) * jnp.dtype(o.dtype).itemsize for o in outs)
    return pl.pallas_call(
        kernel,
        out_shape=out_shape,
        in_specs=in_specs,
        out_specs=jax.tree.map(lambda _: VMEM, out_shape),
        name=name,
        cost_estimate=pl.CostEstimate(flops=flops, bytes_accessed=total, transcendentals=0),
        compiler_params=pltpu.CompilerParams(vmem_limit_bytes=2 * total + (12 << 20)),
    )(*args)


def order_kernel(order_ref, features_ref, grads_ref, out_ref):
    nodes, feat = features_ref.shape
    source = lax.broadcasted_iota(jnp.int32, (nodes, nodes), 0)
    picks = (source == order_ref[...]).astype(jnp.float32).astype(jnp.bfloat16)
    ordered = dot(picks, features_ref[...], ((0,), (0,)))
    out_ref[:, :feat] = ordered.astype(jnp.bfloat16)
    out_ref[:, feat:] = grads_ref[...]


def dense_kernel(blocks, count_ref, rows_ref, cols_ref, tiles_ref, out_ref):
    size = tiles_ref.shape[-1]
    own = lax.axis_index("row")
    out_ref[...] = jnp.zeros_like(out_ref)

    def place(slot, carry):
        column = cols_ref[0, slot]
        piece = lax.bitwise_xor(column // blocks, own)
        row_at = pl.multiple_of(rows_ref[0, slot] * size, size)
        col_at = pl.multiple_of((piece * blocks + column % blocks) * size, size)
        out_ref[pl.ds(row_at, size), pl.ds(col_at, size)] = tiles_ref[slot]
        return carry

    lax.fori_loop(0, count_ref[0, 0], place, 0)


def products(dense_ref, pieces, chunk):
    depth = pieces[0].shape[0]
    for start in range(0, dense_ref.shape[0], chunk):
        total = None
        for k, piece in enumerate(pieces):
            term = dot(dense_ref[start : start + chunk, k * depth : (k + 1) * depth], piece[...])
            total = term if total is None else total + term
        yield start, total


def first_kernel(dense_ref, *refs):
    *pieces, out_ref = refs
    for start, total in products(dense_ref, pieces, 128):
        out_ref[start : start + 128, :] = total


def middle_kernel(mine_ref, theirs_ref, first_ref, second_ref, out_ref):
    feat = first_ref.shape[0]
    half = first_ref.shape[1] // 2
    nodes = out_ref.shape[0] // 2
    col = lax.axis_index("col")
    hid_at = pl.ds(pl.multiple_of(col * half, half), half)
    summed = mine_ref[...] + theirs_ref[...]
    aggregated = summed[:, :feat].astype(jnp.bfloat16)
    back = summed[:, feat:].astype(jnp.bfloat16)
    first_half = first_ref[:, hid_at]
    second_half = second_ref[hid_at, :]

    at = pl.ds(pl.multiple_of(col * nodes, nodes), nodes)
    own = (mine_ref[at, :feat] + theirs_ref[at, :feat]).astype(jnp.bfloat16)
    own_pre = dot(own, first_ref[...])
    own_hidden = (own_pre * jax.nn.sigmoid(own_pre)).astype(jnp.bfloat16)
    out_ref[:nodes, :] = dot(own_hidden, second_ref[...]).astype(jnp.bfloat16)

    pre = dot(aggregated, first_half)
    gate = jax.nn.sigmoid(pre)
    hidden = (pre * gate).astype(jnp.bfloat16)
    hidden_grads = dot(back, second_half, ((1,), (1,)))
    pre_grads = (hidden_grads * gate * (1.0 + pre * (1.0 - gate))).astype(jnp.bfloat16)
    out_ref[nodes : nodes + half, :] = dot(hidden, back, ((0,), (0,))).astype(jnp.bfloat16)
    out_ref[nodes + half :, :] = dot(aggregated, pre_grads, ((0,), (0,))).astype(jnp.bfloat16)


def second_kernel(dense_ref, *refs):
    *pieces, keep_ref, send_ref = refs
    nodes = keep_ref.shape[0]
    col = lax.axis_index("col")
    tops = [piece.at[:nodes, :] for piece in pieces]
    for where, ref in ((col, keep_ref), (1 - col, send_ref)):
        slab = dense_ref.at[pl.ds(pl.multiple_of(where * nodes, nodes), nodes), :]
        for start, total in products(slab, tops, 128):
            ref[start : start + 128, :] = total
    grads = pieces[0][nodes:, :].astype(jnp.float32)
    for piece in pieces[1:]:
        grads = grads + piece[nodes:, :].astype(jnp.float32)
    send_ref[nodes:, :] = grads


def last_kernel(scale, keep_ref, sent_ref, theirs_ref, logits_ref, first_ref, second_ref):
    nodes = keep_ref.shape[0]
    half = second_ref.shape[0] // 2
    col = lax.axis_index("col")
    logits_ref[...] = (keep_ref[...] + theirs_ref[:nodes, :]).astype(jnp.bfloat16)
    for where, ref in ((col, sent_ref), (1 - col, theirs_ref)):
        at = pl.ds(pl.multiple_of(where * half, half), half)
        second_ref[at, :] = ref[nodes : nodes + half, :] * scale
        first_ref[:, at] = ref[nodes + half :, :] * scale


def exchange(x, axis, mask):
    size = lax.axis_size(axis)
    return lax.ppermute(x, axis, [(i, i ^ mask) for i in range(size)])


def gather_rows(x):
    size = lax.axis_size("row")
    inner = 1 << ((size.bit_length() - 1) // 2)
    found = {0: x}
    for mask in range(inner, size, inner):
        found[mask] = exchange(x, "row", mask)
    for low in range(1, inner):
        for mask in range(0, size, inner):
            found[mask + low] = exchange(found[mask], "row", low)
    return [found[k] for k in range(size)]


def shards(
    features,
    node_order,
    weight_first,
    weight_second,
    adjacency_tiles,
    tile_rows,
    tile_cols,
    tile_counts,
    logit_grads,
):
    tiles = adjacency_tiles[0, 0]
    size = tiles.shape[-1]
    nodes, feat = features.shape
    hid, classes = weight_second.shape
    rows, cols = lax.axis_size("row"), lax.axis_size("col")
    slab = cols * nodes
    set_nodes = rows * nodes
    shape = jax.ShapeDtypeStruct
    bf16, f32 = jnp.bfloat16, jnp.float32

    source = call(
        order_kernel, shape((nodes, feat + classes), bf16), [VMEM] * 3,
        2 * nodes * nodes * feat, "order", node_order, features, logit_grads,
    )
    dense = call(
        functools.partial(dense_kernel, nodes // size), shape((slab, set_nodes), bf16),
        [SMEM] * 3 + [VMEM], 0, "dense", tile_counts, tile_rows[0], tile_cols[0], tiles,
    )
    pieces = gather_rows(source)
    partial = call(
        first_kernel, shape((slab, feat + classes), f32), [VMEM] * (1 + rows),
        2 * slab * set_nodes * (feat + classes), "first", dense, *pieces,
    )
    theirs = exchange(partial, "col", 1)
    middle = call(
        middle_kernel, shape((nodes + hid, classes), bf16), [VMEM] * 4,
        10 * slab * feat * hid, "middle", partial, theirs, weight_first, weight_second,
    )
    pieces = gather_rows(middle)
    keep, send = call(
        second_kernel, (shape((nodes, classes), f32), shape((nodes + hid, classes), f32)),
        [VMEM] * (1 + rows), 2 * slab * set_nodes * classes, "second", dense, *pieces,
    )
    theirs = exchange(send, "col", 1)
    return call(
        functools.partial(last_kernel, 1.0 / math.sqrt(set_nodes * cols)),
        (shape((nodes, classes), bf16), shape((feat, hid), f32), shape((hid, classes), f32)),
        [VMEM] * 3, 0, "last", keep, send, theirs,
    )


def solution(mesh):
    return jax.shard_map(
        shards,
        mesh=mesh,
        in_specs=(
            P(("groups", "row", "col"), None),
            P(("groups", "row", "col"), None),
            P(),
            P(),
            P(("groups", "row"), "col", None, None, None),
            P(("groups", "row"), "col", None),
            P(("groups", "row"), "col", None),
            P(("groups", "row"), "col"),
            P(("groups", "row", "col"), None),
        ),
        out_specs=(P(("groups", "row", "col"), None), P("groups", None), P("groups", None)),
        check_vma=False,
    )
```

```python
import functools
import math

import jax
import jax.numpy as jnp
from jax import lax
from jax.experimental import pallas as pl
from jax.experimental.pallas import tpu as pltpu
from jax.sharding import PartitionSpec as P

VMEM = pl.BlockSpec(memory_space=pltpu.VMEM)
HBM = pl.BlockSpec(memory_space=pltpu.HBM)


def dot(a, b, contract=((1,), (0,))):
    return lax.dot_general(a, b, (contract, ((), ())), preferred_element_type=jnp.float32)


def call(kernel, out_shape, in_specs, flops, name, *args):
    total = sum(a.size * a.dtype.itemsize for a in args)
    outs = out_shape if isinstance(out_shape, (tuple, list)) else (out_shape,)
    total += sum(math.prod(o.shape) * jnp.dtype(o.dtype).itemsize for o in outs)
    return pl.pallas_call(
        kernel,
        out_shape=out_shape,
        in_specs=in_specs,
        out_specs=jax.tree.map(lambda _: VMEM, out_shape),
        name=name,
        cost_estimate=pl.CostEstimate(flops=flops, bytes_accessed=total, transcendentals=0),
        compiler_params=pltpu.CompilerParams(vmem_limit_bytes=2 * total + (12 << 20)),
    )(*args)


def prepare_kernel(
    blocks, count_ref, order_hbm, features_hbm, grads_hbm, rows_hbm, cols_hbm, tiles_hbm,
    out_ref, dense_ref, order_ref, features_ref, rows_ref, cols_ref, tiles_ref, sems,
):
    feat = features_hbm.shape[1]
    pairs = (
        (rows_hbm, rows_ref), (cols_hbm, cols_ref),
        (order_hbm, order_ref), (features_hbm, features_ref),
        (grads_hbm, out_ref.at[:, feat:]), (tiles_hbm, tiles_ref),
    )
    copies = [pltpu.make_async_copy(*pair, sems.at[i]) for i, pair in enumerate(pairs)]
    for copy in copies:
        copy.start()
    dense_ref[...] = jnp.zeros_like(dense_ref)
    for copy in copies[:5]:
        copy.wait()
    nodes = features_ref.shape[0]
    source = lax.broadcasted_iota(jnp.int32, (nodes, nodes), 0)
    picks = (source == order_ref[...]).astype(jnp.float32).astype(jnp.bfloat16)
    out_ref[:, :feat] = dot(picks, features_ref[...], ((0,), (0,))).astype(jnp.bfloat16)
    copies[5].wait()
    size = tiles_ref.shape[-1]
    own = lax.axis_index("row")

    def place(slot, carry):
        column = cols_ref[0, slot]
        piece = lax.bitwise_xor(column // blocks, own)
        row_at = pl.multiple_of(rows_ref[0, slot] * size, size)
        col_at = pl.multiple_of((piece * blocks + column % blocks) * size, size)
        dense_ref[pl.ds(row_at, size), pl.ds(col_at, size)] = tiles_ref[slot]
        return carry

    lax.fori_loop(0, count_ref[0, 0], place, 0)


def products(dense_ref, pieces, chunk):
    depth = pieces[0].shape[0]
    for start in range(0, dense_ref.shape[0], chunk):
        total = None
        for k, piece in zip(piece_order(len(pieces)), pieces):
            term = dot(dense_ref[start : start + chunk, k * depth : (k + 1) * depth], piece[...])
            total = term if total is None else total + term
        yield start, total


def first_kernel(dense_ref, *refs):
    *pieces, out_ref = refs
    for start, total in products(dense_ref, pieces, 128):
        out_ref[start : start + 128, :] = total


def middle_kernel(mine_ref, theirs_ref, first_ref, second_ref, out_ref):
    feat = first_ref.shape[0]
    half = first_ref.shape[1] // 2
    nodes = out_ref.shape[0] // 2
    col = lax.axis_index("col")
    hid_at = pl.ds(pl.multiple_of(col * half, half), half)
    summed = mine_ref[...] + theirs_ref[...]
    aggregated = summed[:, :feat].astype(jnp.bfloat16)
    back = summed[:, feat:].astype(jnp.bfloat16)
    first_half = first_ref[:, hid_at]
    second_half = second_ref[hid_at, :]

    at = pl.ds(pl.multiple_of(col * nodes, nodes), nodes)
    own = (mine_ref[at, :feat] + theirs_ref[at, :feat]).astype(jnp.bfloat16)
    own_pre = dot(own, first_ref[...])
    own_hidden = (own_pre * jax.nn.sigmoid(own_pre)).astype(jnp.bfloat16)
    out_ref[:nodes, :] = dot(own_hidden, second_ref[...]).astype(jnp.bfloat16)

    pre = dot(aggregated, first_half)
    gate = jax.nn.sigmoid(pre)
    hidden = (pre * gate).astype(jnp.bfloat16)
    hidden_grads = dot(back, second_half, ((1,), (1,)))
    pre_grads = (hidden_grads * gate * (1.0 + pre * (1.0 - gate))).astype(jnp.bfloat16)
    out_ref[nodes : nodes + half, :] = dot(hidden, back, ((0,), (0,))).astype(jnp.bfloat16)
    out_ref[nodes + half :, :] = dot(aggregated, pre_grads, ((0,), (0,))).astype(jnp.bfloat16)


def second_kernel(dense_ref, *refs):
    *pieces, keep_ref, send_ref = refs
    nodes = keep_ref.shape[0]
    col = lax.axis_index("col")
    tops = [piece.at[:nodes, :] for piece in pieces]
    for where, ref in ((col, keep_ref), (1 - col, send_ref)):
        slab = dense_ref.at[pl.ds(pl.multiple_of(where * nodes, nodes), nodes), :]
        for start, total in products(slab, tops, 128):
            ref[start : start + 128, :] = total
    grads = pieces[0][nodes:, :].astype(jnp.float32)
    for piece in pieces[1:]:
        grads = grads + piece[nodes:, :].astype(jnp.float32)
    send_ref[nodes:, :] = grads


def last_kernel(scale, keep_ref, sent_ref, theirs_ref, logits_ref, first_ref, second_ref):
    nodes = keep_ref.shape[0]
    half = second_ref.shape[0] // 2
    col = lax.axis_index("col")
    logits_ref[...] = (keep_ref[...] + theirs_ref[:nodes, :]).astype(jnp.bfloat16)
    for where, ref in ((col, sent_ref), (1 - col, theirs_ref)):
        at = pl.ds(pl.multiple_of(where * half, half), half)
        second_ref[at, :] = ref[nodes : nodes + half, :] * scale
        first_ref[:, at] = ref[nodes + half :, :] * scale


def exchange(x, axis, mask):
    size = lax.axis_size(axis)
    return lax.ppermute(x, axis, [(i, i ^ mask) for i in range(size)])


def gather_rows(x):
    size = lax.axis_size("row")
    near = min(4, size)
    found = {0: x}
    for mask in [*range(near, size, near), *range(1, near)]:
        found[mask] = exchange(x, "row", mask)
    for mask in range(near, size, near):
        for low in range(1, near):
            found[mask + low] = exchange(found[mask], "row", low)
    return found


def piece_order(rows):
    near = min(4, rows)
    far = [k for k in range(rows - 1, near - 1, -1)]
    return [*range(1, near), *far, 0]


def shards(
    features,
    node_order,
    weight_first,
    weight_second,
    adjacency_tiles,
    tile_rows,
    tile_cols,
    tile_counts,
    logit_grads,
):
    tiles = adjacency_tiles[0, 0]
    size = tiles.shape[-1]
    nodes, feat = features.shape
    hid, classes = weight_second.shape
    rows, cols = lax.axis_size("row"), lax.axis_size("col")
    slab = cols * nodes
    set_nodes = rows * nodes
    shape = jax.ShapeDtypeStruct
    bf16, f32 = jnp.bfloat16, jnp.float32

    slots = tiles.shape[0]
    source, dense = pl.pallas_call(
        functools.partial(prepare_kernel, nodes // size),
        out_shape=(shape((nodes, feat + classes), bf16), shape((slab, set_nodes), bf16)),
        in_specs=[pl.BlockSpec(memory_space=pltpu.SMEM)] + [HBM] * 6,
        out_specs=(VMEM, VMEM),
        scratch_shapes=[
            pltpu.VMEM((1, nodes), jnp.int32),
            pltpu.VMEM((nodes, feat), bf16),
            pltpu.SMEM((1, slots), jnp.int32),
            pltpu.SMEM((1, slots), jnp.int32),
            pltpu.VMEM(tiles.shape, bf16),
            pltpu.SemaphoreType.DMA((6,)),
        ],
        name="prepare",
        compiler_params=pltpu.CompilerParams(
            vmem_limit_bytes=4 * tiles.size + 4 * slab * set_nodes + (8 << 20)
        ),
    )(tile_counts, *(
        pltpu.with_memory_space_constraint(x, pltpu.HBM)
        for x in (node_order, features, logit_grads, tile_rows[0], tile_cols[0], tiles)
    ))
    found = gather_rows(source)
    pieces = [found[k] for k in piece_order(rows)]
    partial = call(
        first_kernel, shape((slab, feat + classes), f32), [VMEM] * (1 + rows),
        2 * slab * set_nodes * (feat + classes), "first", dense, *pieces,
    )
    theirs = exchange(partial, "col", 1)
    middle = call(
        middle_kernel, shape((nodes + hid, classes), bf16), [VMEM] * 4,
        10 * slab * feat * hid, "middle", partial, theirs, weight_first, weight_second,
    )
    found = gather_rows(middle)
    pieces = [found[k] for k in piece_order(rows)]
    keep, send = call(
        second_kernel, (shape((nodes, classes), f32), shape((nodes + hid, classes), f32)),
        [VMEM] * (1 + rows), 2 * slab * set_nodes * classes, "second", dense, *pieces,
    )
    theirs = exchange(send, "col", 1)
    return call(
        functools.partial(last_kernel, 1.0 / math.sqrt(set_nodes * cols)),
        (shape((nodes, classes), bf16), shape((feat, hid), f32), shape((hid, classes), f32)),
        [VMEM] * 3, 0, "last", keep, send, theirs,
    )


def solution(mesh):
    return jax.shard_map(
        shards,
        mesh=mesh,
        in_specs=(
            P(("groups", "row", "col"), None),
            P(("groups", "row", "col"), None),
            P(),
            P(),
            P(("groups", "row"), "col", None, None, None),
            P(("groups", "row"), "col", None),
            P(("groups", "row"), "col", None),
            P(("groups", "row"), "col"),
            P(("groups", "row", "col"), None),
        ),
        out_specs=(P(("groups", "row", "col"), None), P("groups", None), P("groups", None)),
        check_vma=False,
    )
```

```python
import functools
import math

import jax
import jax.numpy as jnp
from jax import lax
from jax.experimental import pallas as pl
from jax.experimental.pallas import tpu as pltpu
from jax.sharding import PartitionSpec as P

VMEM = pl.BlockSpec(memory_space=pltpu.VMEM)
HBM = pl.BlockSpec(memory_space=pltpu.HBM)


def dot(a, b, contract=((1,), (0,))):
    return lax.dot_general(a, b, (contract, ((), ())), preferred_element_type=jnp.float32)


def call(kernel, out_shape, in_specs, flops, name, *args):
    total = sum(a.size * a.dtype.itemsize for a in args)
    outs = out_shape if isinstance(out_shape, (tuple, list)) else (out_shape,)
    total += sum(math.prod(o.shape) * jnp.dtype(o.dtype).itemsize for o in outs)
    return pl.pallas_call(
        kernel,
        out_shape=out_shape,
        in_specs=in_specs,
        out_specs=jax.tree.map(lambda _: VMEM, out_shape),
        name=name,
        cost_estimate=pl.CostEstimate(flops=flops, bytes_accessed=total, transcendentals=0),
        compiler_params=pltpu.CompilerParams(vmem_limit_bytes=2 * total + (12 << 20)),
    )(*args)


def load(pairs, sems):
    copies = [pltpu.make_async_copy(*pair, sems.at[i]) for i, pair in enumerate(pairs)]
    for copy in copies:
        copy.start()
    return copies


def order_kernel(order_hbm, features_hbm, grads_hbm, out_ref, order_ref, features_ref, sems):
    nodes, feat = features_ref.shape
    pairs = (
        (order_hbm, order_ref), (features_hbm, features_ref), (grads_hbm, out_ref.at[:, feat:]),
    )
    for copy in load(pairs, sems):
        copy.wait()
    source = lax.broadcasted_iota(jnp.int32, (nodes, nodes), 0)
    picks = (source == order_ref[...]).astype(jnp.float32).astype(jnp.bfloat16)
    out_ref[:, :feat] = dot(picks, features_ref[...], ((0,), (0,))).astype(jnp.bfloat16)


def dense_kernel(
    blocks, count_ref, rows_hbm, cols_hbm, tiles_hbm, dense_ref, rows_ref, cols_ref, tiles_ref, sems
):
    copies = load(((rows_hbm, rows_ref), (cols_hbm, cols_ref), (tiles_hbm, tiles_ref)), sems)
    dense_ref[...] = jnp.zeros_like(dense_ref)
    for copy in copies:
        copy.wait()
    size = tiles_ref.shape[-1]
    own = lax.axis_index("row")

    def place(slot, carry):
        column = cols_ref[0, slot]
        piece = lax.bitwise_xor(column // blocks, own)
        row_at = pl.multiple_of(rows_ref[0, slot] * size, size)
        col_at = pl.multiple_of((piece * blocks + column % blocks) * size, size)
        dense_ref[pl.ds(row_at, size), pl.ds(col_at, size)] = tiles_ref[slot]
        return carry

    lax.fori_loop(0, count_ref[0, 0], place, 0)


def products(dense_ref, masks, pieces, chunk):
    depth = pieces[0].shape[0]
    for start in range(0, dense_ref.shape[0], chunk):
        total = None
        for k, piece in zip(masks, pieces):
            term = dot(dense_ref[start : start + chunk, k * depth : (k + 1) * depth], piece[...])
            total = term if total is None else total + term
        yield start, total


def early_kernel(masks, dense_ref, *refs):
    *pieces, out_ref = refs
    for start, total in products(dense_ref, masks, pieces, 128):
        out_ref[start : start + 128, :] = total


def first_kernel(masks, dense_ref, early_ref, *refs):
    *pieces, out_ref = refs
    for start, total in products(dense_ref, masks, pieces, 128):
        at = slice(start, start + 128)
        out_ref[at, :] = total + early_ref[at, :]


def middle_kernel(mine_ref, theirs_ref, first_ref, second_ref, out_ref):
    feat = first_ref.shape[0]
    half = first_ref.shape[1] // 2
    nodes = out_ref.shape[0] // 2
    col = lax.axis_index("col")
    hid_at = pl.ds(pl.multiple_of(col * half, half), half)
    summed = mine_ref[...] + theirs_ref[...]
    aggregated = summed[:, :feat].astype(jnp.bfloat16)
    back = summed[:, feat:].astype(jnp.bfloat16)
    first_half = first_ref[:, hid_at]
    second_half = second_ref[hid_at, :]

    at = pl.ds(pl.multiple_of(col * nodes, nodes), nodes)
    own = mine_ref[at, :feat] + theirs_ref[at, :feat]
    own_pre = dot(own.astype(jnp.bfloat16), first_ref[...])
    own_hidden = (own_pre * jax.nn.sigmoid(own_pre)).astype(jnp.bfloat16)
    out_ref[:nodes, :] = dot(own_hidden, second_ref[...]).astype(jnp.bfloat16)

    pre = dot(aggregated, first_half)
    gate = jax.nn.sigmoid(pre)
    hidden = (pre * gate).astype(jnp.bfloat16)
    hidden_grads = dot(back, second_half, ((1,), (1,)))
    pre_grads = (hidden_grads * gate * (1.0 + pre * (1.0 - gate))).astype(jnp.bfloat16)
    out_ref[nodes : nodes + half, :] = dot(hidden, back, ((0,), (0,))).astype(jnp.bfloat16)
    out_ref[nodes + half :, :] = dot(aggregated, pre_grads, ((0,), (0,))).astype(jnp.bfloat16)


def early_logits_kernel(masks, dense_ref, *refs):
    *pieces, out_ref = refs
    slab = dense_ref.shape[0]
    nodes = slab // 2
    tops = [piece.at[:nodes, :] for piece in pieces]
    for start, total in products(dense_ref, masks, tops, 128):
        out_ref[start : start + 128, :] = total
    grads = pieces[0][nodes:, :].astype(jnp.float32)
    for piece in pieces[1:]:
        grads = grads + piece[nodes:, :].astype(jnp.float32)
    out_ref[slab:, :] = grads


def second_kernel(masks, dense_ref, early_ref, *refs):
    *pieces, keep_ref, send_ref = refs
    nodes = keep_ref.shape[0]
    col = lax.axis_index("col")
    tops = [piece.at[:nodes, :] for piece in pieces]
    for where, ref in ((col, keep_ref), (1 - col, send_ref)):
        at = pl.ds(pl.multiple_of(where * nodes, nodes), nodes)
        early = early_ref.at[at, :]
        for start, total in products(dense_ref.at[at, :], masks, tops, 128):
            ref[start : start + 128, :] = total + early[start : start + 128, :]
    grads = early_ref[2 * nodes :, :]
    for piece in pieces:
        grads = grads + piece[nodes:, :].astype(jnp.float32)
    send_ref[nodes:, :] = grads


def last_kernel(scale, keep_ref, sent_ref, theirs_ref, logits_ref, first_ref, second_ref):
    nodes = keep_ref.shape[0]
    half = second_ref.shape[0] // 2
    col = lax.axis_index("col")
    logits_ref[...] = (keep_ref[...] + theirs_ref[:nodes, :]).astype(jnp.bfloat16)
    for where, ref in ((col, sent_ref), (1 - col, theirs_ref)):
        at = pl.ds(pl.multiple_of(where * half, half), half)
        second_ref[at, :] = ref[nodes : nodes + half, :] * scale
        first_ref[:, at] = ref[nodes + half :, :] * scale


def exchange(x, axis, mask):
    size = lax.axis_size(axis)
    return lax.ppermute(x, axis, [(i, i ^ mask) for i in range(size)])


def gather_rows(x):
    size = lax.axis_size("row")
    near = min(4, size)
    found = {0: x}
    for mask in [*range(near, size, near), *range(1, near)]:
        found[mask] = exchange(x, "row", mask)
    for mask in range(near, size, near):
        for low in range(1, near):
            found[mask + low] = exchange(found[mask], "row", low)
    return found


def arrival(rows):
    near = min(4, rows)
    far = [*range(near, rows, near)]
    last = [mask + low for mask in far for low in (2, 3, 1) if low < near]
    return [*range(1, near), *far, 0], last


def shards(
    features,
    node_order,
    weight_first,
    weight_second,
    adjacency_tiles,
    tile_rows,
    tile_cols,
    tile_counts,
    logit_grads,
):
    tiles = adjacency_tiles[0, 0]
    size = tiles.shape[-1]
    nodes, feat = features.shape
    hid, classes = weight_second.shape
    rows, cols = lax.axis_size("row"), lax.axis_size("col")
    slab = cols * nodes
    set_nodes = rows * nodes
    shape = jax.ShapeDtypeStruct
    bf16, f32 = jnp.bfloat16, jnp.float32

    slots = tiles.shape[0]
    in_hbm = functools.partial(pltpu.with_memory_space_constraint, memory_space=pltpu.HBM)
    source = pl.pallas_call(
        order_kernel,
        out_shape=shape((nodes, feat + classes), bf16),
        in_specs=[HBM] * 3,
        out_specs=VMEM,
        scratch_shapes=[
            pltpu.VMEM((1, nodes), jnp.int32),
            pltpu.VMEM((nodes, feat), bf16),
            pltpu.SemaphoreType.DMA((3,)),
        ],
        name="order",
        compiler_params=pltpu.CompilerParams(vmem_limit_bytes=8 << 20),
    )(in_hbm(node_order), in_hbm(features), in_hbm(logit_grads))
    dense = pl.pallas_call(
        functools.partial(dense_kernel, nodes // size),
        out_shape=shape((slab, set_nodes), bf16),
        in_specs=[pl.BlockSpec(memory_space=pltpu.SMEM)] + [HBM] * 3,
        out_specs=VMEM,
        scratch_shapes=[
            pltpu.SMEM((1, slots), jnp.int32),
            pltpu.SMEM((1, slots), jnp.int32),
            pltpu.VMEM(tiles.shape, bf16),
            pltpu.SemaphoreType.DMA((3,)),
        ],
        name="dense",
        compiler_params=pltpu.CompilerParams(
            vmem_limit_bytes=4 * tiles.size + 4 * slab * set_nodes + (8 << 20)
        ),
    )(tile_counts, in_hbm(tile_rows[0]), in_hbm(tile_cols[0]), in_hbm(tiles))

    early, late = arrival(rows)
    flops = 2 * slab * nodes * (feat + classes)
    found = gather_rows(source)
    partial = call(
        functools.partial(early_kernel, early), shape((slab, feat + classes), f32),
        [VMEM] * (1 + len(early)), flops * len(early), "early", dense, *(found[k] for k in early),
    )
    mine = call(
        functools.partial(first_kernel, late), shape((slab, feat + classes), f32),
        [VMEM] * (2 + len(late)), flops * len(late), "first",
        dense, partial, *(found[k] for k in late),
    )
    middle = call(
        middle_kernel, shape((nodes + hid, classes), bf16), [VMEM] * 4, 10 * slab * feat * hid,
        "middle", mine, exchange(mine, "col", 1), weight_first, weight_second,
    )
    flops = 2 * slab * nodes * classes
    found = gather_rows(middle)
    partial = call(
        functools.partial(early_logits_kernel, early), shape((slab + hid, classes), f32),
        [VMEM] * (1 + len(early)), flops * len(early), "early_logits",
        dense, *(found[k] for k in early),
    )
    keep, send = call(
        functools.partial(second_kernel, late),
        (shape((nodes, classes), f32), shape((nodes + hid, classes), f32)),
        [VMEM] * (2 + len(late)), flops * len(late), "second",
        dense, partial, *(found[k] for k in late),
    )
    theirs = exchange(send, "col", 1)
    return call(
        functools.partial(last_kernel, 1.0 / math.sqrt(set_nodes * cols)),
        (shape((nodes, classes), bf16), shape((feat, hid), f32), shape((hid, classes), f32)),
        [VMEM] * 3, 0, "last", keep, send, theirs,
    )


def solution(mesh):
    return jax.shard_map(
        shards,
        mesh=mesh,
        in_specs=(
            P(("groups", "row", "col"), None),
            P(("groups", "row", "col"), None),
            P(),
            P(),
            P(("groups", "row"), "col", None, None, None),
            P(("groups", "row"), "col", None),
            P(("groups", "row"), "col", None),
            P(("groups", "row"), "col"),
            P(("groups", "row", "col"), None),
        ),
        out_specs=(P(("groups", "row", "col"), None), P("groups", None), P("groups", None)),
        check_vma=False,
    )
```

```python
import functools
import math

import jax
import jax.numpy as jnp
from jax import lax
from jax.experimental import pallas as pl
from jax.experimental.pallas import tpu as pltpu
from jax.sharding import PartitionSpec as P

VMEM = pl.BlockSpec(memory_space=pltpu.VMEM)
HBM = pl.BlockSpec(memory_space=pltpu.HBM)


def dot(a, b, contract=((1,), (0,))):
    return lax.dot_general(a, b, (contract, ((), ())), preferred_element_type=jnp.float32)


def call(kernel, out_shape, in_specs, flops, name, *args):
    total = sum(a.size * a.dtype.itemsize for a in args)
    outs = out_shape if isinstance(out_shape, (tuple, list)) else (out_shape,)
    total += sum(math.prod(o.shape) * jnp.dtype(o.dtype).itemsize for o in outs)
    return pl.pallas_call(
        kernel,
        out_shape=out_shape,
        in_specs=in_specs,
        out_specs=jax.tree.map(lambda _: VMEM, out_shape),
        name=name,
        cost_estimate=pl.CostEstimate(flops=flops, bytes_accessed=total, transcendentals=0),
        compiler_params=pltpu.CompilerParams(vmem_limit_bytes=2 * total + (12 << 20)),
    )(*args)


def load(pairs, sems):
    copies = [pltpu.make_async_copy(*pair, sems.at[i]) for i, pair in enumerate(pairs)]
    for copy in copies:
        copy.start()
    return copies


def order_kernel(order_hbm, features_hbm, grads_hbm, out_ref, order_ref, features_ref, sems):
    nodes, feat = features_ref.shape
    pairs = (
        (order_hbm, order_ref), (features_hbm, features_ref), (grads_hbm, out_ref.at[:, feat:]),
    )
    for copy in load(pairs, sems):
        copy.wait()
    source = lax.broadcasted_iota(jnp.int32, (nodes, nodes), 0)
    picks = (source == order_ref[...]).astype(jnp.float32).astype(jnp.bfloat16)
    out_ref[:, :feat] = dot(picks, features_ref[...], ((0,), (0,))).astype(jnp.bfloat16)


def dense_kernel(
    blocks, count_ref, rows_hbm, cols_hbm, tiles_hbm, dense_ref, rows_ref, cols_ref, tiles_ref, sems
):
    copies = load(((rows_hbm, rows_ref), (cols_hbm, cols_ref), (tiles_hbm, tiles_ref)), sems)
    dense_ref[...] = jnp.zeros_like(dense_ref)
    for copy in copies:
        copy.wait()
    size = tiles_ref.shape[-1]
    own = lax.axis_index("row")

    def place(slot, carry):
        column = cols_ref[0, slot]
        piece = lax.bitwise_xor(column // blocks, own)
        row_at = pl.multiple_of(rows_ref[0, slot] * size, size)
        col_at = pl.multiple_of((piece * blocks + column % blocks) * size, size)
        dense_ref[pl.ds(row_at, size), pl.ds(col_at, size)] = tiles_ref[slot]
        return carry

    lax.fori_loop(0, count_ref[0, 0], place, 0)


def products(dense_ref, masks, pieces, chunk):
    depth = pieces[0].shape[0]
    for start in range(0, dense_ref.shape[0], chunk):
        total = None
        for k, piece in zip(masks, pieces):
            term = dot(dense_ref[start : start + chunk, k * depth : (k + 1) * depth], piece[...])
            total = term if total is None else total + term
        yield start, total


def early_kernel(masks, dense_ref, *refs):
    *pieces, out_ref = refs
    for start, total in products(dense_ref, masks, pieces, 128):
        out_ref[start : start + 128, :] = total


def first_kernel(masks, dense_ref, early_ref, *refs):
    *pieces, out_ref = refs
    for start, total in products(dense_ref, masks, pieces, 128):
        at = slice(start, start + 128)
        out_ref[at, :] = total + early_ref[at, :]


def middle_kernel(mine_ref, theirs_ref, first_ref, second_ref, out_ref):
    feat = first_ref.shape[0]
    half = first_ref.shape[1] // 2
    nodes = out_ref.shape[0] // 2
    col = lax.axis_index("col")
    hid_at = pl.ds(pl.multiple_of(col * half, half), half)
    summed = mine_ref[...] + theirs_ref[...]
    aggregated = summed[:, :feat].astype(jnp.bfloat16)
    back = summed[:, feat:].astype(jnp.bfloat16)
    first_half = first_ref[:, hid_at]
    second_half = second_ref[hid_at, :]

    at = pl.ds(pl.multiple_of(col * nodes, nodes), nodes)
    own = mine_ref[at, :feat] + theirs_ref[at, :feat]
    own_pre = dot(own.astype(jnp.bfloat16), first_ref[...])
    own_hidden = (own_pre * jax.nn.sigmoid(own_pre)).astype(jnp.bfloat16)
    out_ref[:nodes, :] = dot(own_hidden, second_ref[...]).astype(jnp.bfloat16)

    pre = dot(aggregated, first_half)
    gate = jax.nn.sigmoid(pre)
    hidden = (pre * gate).astype(jnp.bfloat16)
    hidden_grads = dot(back, second_half, ((1,), (1,)))
    pre_grads = (hidden_grads * gate * (1.0 + pre * (1.0 - gate))).astype(jnp.bfloat16)
    out_ref[nodes : nodes + half, :] = dot(hidden, back, ((0,), (0,))).astype(jnp.bfloat16)
    out_ref[nodes + half :, :] = dot(aggregated, pre_grads, ((0,), (0,))).astype(jnp.bfloat16)


def early_logits_kernel(masks, dense_ref, *refs):
    *pieces, out_ref = refs
    slab = dense_ref.shape[0]
    nodes = slab // 2
    tops = [piece.at[:nodes, :] for piece in pieces]
    for start, total in products(dense_ref, masks, tops, 128):
        out_ref[start : start + 128, :] = total
    grads = pieces[0][nodes:, :].astype(jnp.float32)
    for piece in pieces[1:]:
        grads = grads + piece[nodes:, :].astype(jnp.float32)
    out_ref[slab:, :] = grads


def second_kernel(masks, dense_ref, early_ref, *refs):
    *pieces, keep_ref, send_ref = refs
    nodes = keep_ref.shape[0]
    col = lax.axis_index("col")
    tops = [piece.at[:nodes, :] for piece in pieces]
    for where, ref in ((col, keep_ref), (1 - col, send_ref)):
        at = pl.ds(pl.multiple_of(where * nodes, nodes), nodes)
        early = early_ref.at[at, :]
        for start, total in products(dense_ref.at[at, :], masks, tops, 128):
            ref[start : start + 128, :] = total + early[start : start + 128, :]
    grads = early_ref[2 * nodes :, :]
    for piece in pieces:
        grads = grads + piece[nodes:, :].astype(jnp.float32)
    send_ref[nodes:, :] = grads


def last_kernel(scale, keep_ref, sent_ref, theirs_ref, logits_ref, first_ref, second_ref):
    nodes = keep_ref.shape[0]
    half = second_ref.shape[0] // 2
    col = lax.axis_index("col")
    logits_ref[...] = (keep_ref[...] + theirs_ref[:nodes, :]).astype(jnp.bfloat16)
    for where, ref in ((col, sent_ref), (1 - col, theirs_ref)):
        at = pl.ds(pl.multiple_of(where * half, half), half)
        second_ref[at, :] = ref[nodes : nodes + half, :] * scale
        first_ref[:, at] = ref[nodes + half :, :] * scale


def exchange(x, axis, mask):
    size = lax.axis_size(axis)
    return lax.ppermute(x, axis, [(i, i ^ mask) for i in range(size)])


def gather_rows(x):
    size = lax.axis_size("row")
    near = min(4, size)
    found = {0: x}
    for mask in [*range(near, size, near), *range(1, near)]:
        found[mask] = exchange(x, "row", mask)
    for mask in range(near, size, near):
        for low in range(1, near):
            found[mask + low] = exchange(found[mask], "row", low)
    return found


def arrival(rows):
    near = min(4, rows)
    far = [*range(near, rows, near)]
    order = [low for low in (3, 1, 2) if low < near]
    return [*order, *far, 0], [mask + low for mask in far for low in order]


def shards(
    features,
    node_order,
    weight_first,
    weight_second,
    adjacency_tiles,
    tile_rows,
    tile_cols,
    tile_counts,
    logit_grads,
):
    tiles = adjacency_tiles[0, 0]
    size = tiles.shape[-1]
    nodes, feat = features.shape
    hid, classes = weight_second.shape
    rows, cols = lax.axis_size("row"), lax.axis_size("col")
    slab = cols * nodes
    set_nodes = rows * nodes
    shape = jax.ShapeDtypeStruct
    bf16, f32 = jnp.bfloat16, jnp.float32

    slots = tiles.shape[0]
    in_hbm = functools.partial(pltpu.with_memory_space_constraint, memory_space=pltpu.HBM)
    source = pl.pallas_call(
        order_kernel,
        out_shape=shape((nodes, feat + classes), bf16),
        in_specs=[HBM] * 3,
        out_specs=VMEM,
        scratch_shapes=[
            pltpu.VMEM((1, nodes), jnp.int32),
            pltpu.VMEM((nodes, feat), bf16),
            pltpu.SemaphoreType.DMA((3,)),
        ],
        name="order",
        compiler_params=pltpu.CompilerParams(vmem_limit_bytes=8 << 20),
    )(in_hbm(node_order), in_hbm(features), in_hbm(logit_grads))
    dense = pl.pallas_call(
        functools.partial(dense_kernel, nodes // size),
        out_shape=shape((slab, set_nodes), bf16),
        in_specs=[pl.BlockSpec(memory_space=pltpu.SMEM)] + [HBM] * 3,
        out_specs=VMEM,
        scratch_shapes=[
            pltpu.SMEM((1, slots), jnp.int32),
            pltpu.SMEM((1, slots), jnp.int32),
            pltpu.VMEM(tiles.shape, bf16),
            pltpu.SemaphoreType.DMA((3,)),
        ],
        name="dense",
        compiler_params=pltpu.CompilerParams(
            vmem_limit_bytes=4 * tiles.size + 4 * slab * set_nodes + (8 << 20)
        ),
    )(tile_counts, in_hbm(tile_rows[0]), in_hbm(tile_cols[0]), in_hbm(tiles))

    early, late = arrival(rows)
    flops = 2 * slab * nodes * (feat + classes)
    found = gather_rows(source)
    partial = call(
        functools.partial(early_kernel, early), shape((slab, feat + classes), f32),
        [VMEM] * (1 + len(early)), flops * len(early), "early", dense, *(found[k] for k in early),
    )
    mine = call(
        functools.partial(first_kernel, late), shape((slab, feat + classes), f32),
        [VMEM] * (2 + len(late)), flops * len(late), "first",
        dense, partial, *(found[k] for k in late),
    )
    middle = call(
        middle_kernel, shape((nodes + hid, classes), bf16), [VMEM] * 4, 10 * slab * feat * hid,
        "middle", mine, exchange(mine, "col", 1), weight_first, weight_second,
    )
    flops = 2 * slab * nodes * classes
    found = gather_rows(middle)
    partial = call(
        functools.partial(early_logits_kernel, early), shape((slab + hid, classes), f32),
        [VMEM] * (1 + len(early)), flops * len(early), "early_logits",
        dense, *(found[k] for k in early),
    )
    keep, send = call(
        functools.partial(second_kernel, late),
        (shape((nodes, classes), f32), shape((nodes + hid, classes), f32)),
        [VMEM] * (2 + len(late)), flops * len(late), "second",
        dense, partial, *(found[k] for k in late),
    )
    theirs = exchange(send, "col", 1)
    return call(
        functools.partial(last_kernel, 1.0 / math.sqrt(set_nodes * cols)),
        (shape((nodes, classes), bf16), shape((feat, hid), f32), shape((hid, classes), f32)),
        [VMEM] * 3, 0, "last", keep, send, theirs,
    )


def solution(mesh):
    return jax.shard_map(
        shards,
        mesh=mesh,
        in_specs=(
            P(("groups", "row", "col"), None),
            P(("groups", "row", "col"), None),
            P(),
            P(),
            P(("groups", "row"), "col", None, None, None),
            P(("groups", "row"), "col", None),
            P(("groups", "row"), "col", None),
            P(("groups", "row"), "col"),
            P(("groups", "row", "col"), None),
        ),
        out_specs=(P(("groups", "row", "col"), None), P("groups", None), P("groups", None)),
        check_vma=False,
    )
```

```python
import functools
import math

import jax
import jax.numpy as jnp
from jax import lax
from jax.experimental import pallas as pl
from jax.experimental.pallas import tpu as pltpu
from jax.sharding import PartitionSpec as P

VMEM = pl.BlockSpec(memory_space=pltpu.VMEM)
HBM = pl.BlockSpec(memory_space=pltpu.HBM)


def dot(a, b, contract=((1,), (0,))):
    return lax.dot_general(a, b, (contract, ((), ())), preferred_element_type=jnp.float32)


def call(kernel, out_shape, in_specs, flops, name, *args):
    total = sum(a.size * a.dtype.itemsize for a in args)
    outs = out_shape if isinstance(out_shape, (tuple, list)) else (out_shape,)
    total += sum(math.prod(o.shape) * jnp.dtype(o.dtype).itemsize for o in outs)
    return pl.pallas_call(
        kernel,
        out_shape=out_shape,
        in_specs=in_specs,
        out_specs=jax.tree.map(lambda _: VMEM, out_shape),
        name=name,
        cost_estimate=pl.CostEstimate(flops=flops, bytes_accessed=total, transcendentals=0),
        compiler_params=pltpu.CompilerParams(vmem_limit_bytes=2 * total + (12 << 20)),
    )(*args)


def load(pairs, sems):
    copies = [pltpu.make_async_copy(*pair, sems.at[i]) for i, pair in enumerate(pairs)]
    for copy in copies:
        copy.start()
    return copies


def order_kernel(order_hbm, features_hbm, grads_hbm, out_ref, order_ref, features_ref, sems):
    nodes, feat = features_ref.shape
    pairs = (
        (order_hbm, order_ref), (features_hbm, features_ref), (grads_hbm, out_ref.at[:, feat:]),
    )
    for copy in load(pairs, sems):
        copy.wait()
    source = lax.broadcasted_iota(jnp.int32, (nodes, nodes), 0)
    picks = (source == order_ref[...]).astype(jnp.float32).astype(jnp.bfloat16)
    out_ref[:, :feat] = dot(picks, features_ref[...], ((0,), (0,))).astype(jnp.bfloat16)


def dense_kernel(
    blocks, count_ref, rows_hbm, cols_hbm, tiles_hbm, dense_ref, rows_ref, cols_ref, tiles_ref, sems
):
    copies = load(((rows_hbm, rows_ref), (cols_hbm, cols_ref), (tiles_hbm, tiles_ref)), sems)
    dense_ref[...] = jnp.zeros_like(dense_ref)
    for copy in copies:
        copy.wait()
    size = tiles_ref.shape[-1]
    own = lax.axis_index("row")

    def place(slot, carry):
        column = cols_ref[0, slot]
        piece = lax.bitwise_xor(column // blocks, own)
        row_at = pl.multiple_of(rows_ref[0, slot] * size, size)
        col_at = pl.multiple_of((piece * blocks + column % blocks) * size, size)
        dense_ref[pl.ds(row_at, size), pl.ds(col_at, size)] = tiles_ref[slot]
        return carry

    lax.fori_loop(0, count_ref[0, 0], place, 0)


def products(dense_ref, masks, pieces, chunk):
    depth = pieces[0].shape[0]
    for start in range(0, dense_ref.shape[0], chunk):
        total = None
        for k, piece in zip(masks, pieces):
            term = dot(dense_ref[start : start + chunk, k * depth : (k + 1) * depth], piece[...])
            total = term if total is None else total + term
        yield start, total


def early_kernel(masks, dense_ref, *refs):
    *pieces, out_ref = refs
    for start, total in products(dense_ref, masks, pieces, 128):
        out_ref[start : start + 128, :] = total


def first_kernel(masks, dense_ref, early_ref, *refs):
    *pieces, out_ref = refs
    for start, total in products(dense_ref, masks, pieces, 128):
        at = slice(start, start + 128)
        out_ref[at, :] = total + early_ref[at, :]


def middle_kernel(mine_ref, theirs_ref, first_ref, second_ref, projected_ref, out_ref):
    feat = first_ref.shape[0]
    half = first_ref.shape[1] // 2
    nodes = projected_ref.shape[0]
    col = lax.axis_index("col")
    hid_at = pl.ds(pl.multiple_of(col * half, half), half)
    summed = mine_ref[...] + theirs_ref[...]
    aggregated = summed[:, :feat].astype(jnp.bfloat16)
    back = summed[:, feat:].astype(jnp.bfloat16)
    first_half = first_ref[:, hid_at]
    second_half = second_ref[hid_at, :]

    at = pl.ds(pl.multiple_of(col * nodes, nodes), nodes)
    own = mine_ref[at, :feat] + theirs_ref[at, :feat]
    own_pre = dot(own.astype(jnp.bfloat16), first_ref[...])
    own_hidden = (own_pre * jax.nn.sigmoid(own_pre)).astype(jnp.bfloat16)
    projected = dot(own_hidden, second_ref[...]).astype(jnp.bfloat16)
    projected_ref[...] = projected
    out_ref[:nodes, :] = projected

    pre = dot(aggregated, first_half)
    gate = jax.nn.sigmoid(pre)
    hidden = (pre * gate).astype(jnp.bfloat16)
    hidden_grads = dot(back, second_half, ((1,), (1,)))
    pre_grads = (hidden_grads * gate * (1.0 + pre * (1.0 - gate))).astype(jnp.bfloat16)
    out_ref[nodes : nodes + half, :] = dot(hidden, back, ((0,), (0,))).astype(jnp.bfloat16)
    out_ref[nodes + half :, :] = dot(aggregated, pre_grads, ((0,), (0,))).astype(jnp.bfloat16)


def early_logits_kernel(masks, dense_ref, *refs):
    *pieces, out_ref = refs
    nodes = out_ref.shape[0] // 2
    early_kernel(masks, dense_ref, *(piece.at[:nodes, :] for piece in pieces), out_ref)


def more_logits_kernel(masks, dense_ref, early_ref, *refs):
    *pieces, out_ref = refs
    nodes = out_ref.shape[0] // 2
    tops = (piece.at[:nodes, :] for piece in pieces)
    first_kernel(masks, dense_ref, early_ref, *tops, out_ref)


def sum_kernel(*refs):
    *parts, out_ref = refs
    at = slice(parts[0].shape[0] - out_ref.shape[0], None)
    total = parts[0][at, :].astype(jnp.float32)
    for part in parts[1:]:
        total = total + part[at, :].astype(jnp.float32)
    out_ref[...] = total.astype(jnp.bfloat16)


def second_kernel(masks, dense_ref, early_ref, *refs):
    *pieces, keep_ref, send_ref = refs
    nodes = keep_ref.shape[0]
    col = lax.axis_index("col")
    for where, ref in ((col, keep_ref), (1 - col, send_ref)):
        at = pl.ds(pl.multiple_of(where * nodes, nodes), nodes)
        early = early_ref.at[at, :]
        for start, total in products(dense_ref.at[at, :], masks, pieces, 128):
            ref[start : start + 128, :] = total + early[start : start + 128, :]


def last_kernel(scale, keep_ref, their_logits_ref, *refs):
    *parts, logits_ref, first_ref, second_ref = refs
    logits_ref[...] = (keep_ref[...] + their_logits_ref[...]).astype(jnp.bfloat16)
    half = second_ref.shape[0] // 2
    col = lax.axis_index("col")
    count = len(parts) // 2
    for where, some in ((col, parts[:count]), (1 - col, parts[count:])):
        total = some[0][...].astype(jnp.float32)
        for part in some[1:]:
            total = total + part[...].astype(jnp.float32)
        at = pl.ds(pl.multiple_of(where * half, half), half)
        second_ref[at, :] = total[:half, :] * scale
        first_ref[:, at] = total[half:, :] * scale


def exchange(x, axis, mask):
    size = lax.axis_size(axis)
    return lax.ppermute(x, axis, [(i, i ^ mask) for i in range(size)])


def near_size():
    return min(4, lax.axis_size("row"))


def from_far(x):
    size = lax.axis_size("row")
    return {mask: exchange(x, "row", mask) for mask in range(near_size(), size, near_size())}


def from_near(x, far):
    found = {low: exchange(x, "row", low) for low in range(1, near_size())}
    for mask, block in far.items():
        for low in range(1, near_size()):
            found[mask + low] = exchange(block, "row", low)
    return found


def arrival(near_order, last_order):
    size, near = lax.axis_size("row"), near_size()
    far = [*range(near, size, near)]
    first = [low for low in near_order if low < near]
    last = [mask + low for mask in far for low in last_order if low < near]
    return first, [*far, 0], last


def shards(
    features,
    node_order,
    weight_first,
    weight_second,
    adjacency_tiles,
    tile_rows,
    tile_cols,
    tile_counts,
    logit_grads,
):
    tiles = adjacency_tiles[0, 0]
    size = tiles.shape[-1]
    nodes, feat = features.shape
    hid, classes = weight_second.shape
    rows, cols = lax.axis_size("row"), lax.axis_size("col")
    slab = cols * nodes
    set_nodes = rows * nodes
    shape = jax.ShapeDtypeStruct
    bf16, f32 = jnp.bfloat16, jnp.float32

    slots = tiles.shape[0]
    in_hbm = functools.partial(pltpu.with_memory_space_constraint, memory_space=pltpu.HBM)
    source = pl.pallas_call(
        order_kernel,
        out_shape=shape((nodes, feat + classes), bf16),
        in_specs=[HBM] * 3,
        out_specs=VMEM,
        scratch_shapes=[
            pltpu.VMEM((1, nodes), jnp.int32),
            pltpu.VMEM((nodes, feat), bf16),
            pltpu.SemaphoreType.DMA((3,)),
        ],
        name="order",
        compiler_params=pltpu.CompilerParams(vmem_limit_bytes=8 << 20),
    )(in_hbm(node_order), in_hbm(features), in_hbm(logit_grads))
    dense = pl.pallas_call(
        functools.partial(dense_kernel, nodes // size),
        out_shape=shape((slab, set_nodes), bf16),
        in_specs=[pl.BlockSpec(memory_space=pltpu.SMEM)] + [HBM] * 3,
        out_specs=VMEM,
        scratch_shapes=[
            pltpu.SMEM((1, slots), jnp.int32),
            pltpu.SMEM((1, slots), jnp.int32),
            pltpu.VMEM(tiles.shape, bf16),
            pltpu.SemaphoreType.DMA((3,)),
        ],
        name="dense",
        cost_estimate=pl.CostEstimate(flops=1 * 10**6, bytes_accessed=4 * tiles.size, transcendentals=0),
        compiler_params=pltpu.CompilerParams(
            vmem_limit_bytes=4 * tiles.size + 4 * slab * set_nodes + (8 << 20)
        ),
    )(tile_counts, in_hbm(tile_rows[0]), in_hbm(tile_cols[0]), in_hbm(tiles))

    near, direct, late = arrival((3, 1, 2), (3, 1, 2))
    early = near + direct
    flops = 2 * slab * nodes * (feat + classes)
    far = from_far(source)
    found = {0: source} | far | from_near(source, far)
    partial = call(
        functools.partial(early_kernel, early), shape((slab, feat + classes), f32),
        [VMEM] * (1 + len(early)), 1 * 10**6, "early", dense, *(found[k] for k in early),
    )
    mine = call(
        functools.partial(first_kernel, late), shape((slab, feat + classes), f32),
        [VMEM] * (2 + len(late)), 40000 * 10**6, "first",
        dense, partial, *(found[k] for k in late),
    )
    projected, both = call(
        middle_kernel, (shape((nodes, classes), bf16), shape((nodes + hid, classes), bf16)),
        [VMEM] * 4, 10 * slab * feat * hid,
        "middle", mine, exchange(mine, "col", 1), weight_first, weight_second,
    )
    flops = 2 * slab * nodes * classes
    far = from_far(projected)
    found = {0: both} | far | from_near(both, far)
    near, direct, late = arrival((2, 3, 1), (2, 3, 1))
    partial = call(
        functools.partial(early_logits_kernel, direct), shape((slab, classes), f32),
        [VMEM] * (1 + len(direct)), 15000 * 10**6, "early_logits", dense, *(found[k] for k in direct),
    )
    partial = call(
        functools.partial(more_logits_kernel, near), shape((slab, classes), f32),
        [VMEM] * (2 + len(near)), 1 * 10**6, "more_logits", dense, partial, *(found[k] for k in near),
    )
    keep, send = call(
        functools.partial(second_kernel, late), (shape((nodes, classes), f32),) * 2,
        [VMEM] * (2 + len(late)), 1 * 10**6, "second",
        dense, partial, *(found[k] for k in late),
    )
    parts = [found[low] for low in range(near_size())]
    total = call(
        sum_kernel, shape((hid, classes), bf16), [VMEM] * len(parts), 0, "sum", *parts
    )
    sums = [total, *from_far(total).values()]
    return call(
        functools.partial(last_kernel, 1.0 / math.sqrt(set_nodes * cols)),
        (shape((nodes, classes), bf16), shape((feat, hid), f32), shape((hid, classes), f32)),
        [VMEM] * (2 + 2 * len(sums)), 0, "last",
        keep, exchange(send, "col", 1), *sums, *(exchange(x, "col", 1) for x in sums),
    )


def solution(mesh):
    return jax.shard_map(
        shards,
        mesh=mesh,
        in_specs=(
            P(("groups", "row", "col"), None),
            P(("groups", "row", "col"), None),
            P(),
            P(),
            P(("groups", "row"), "col", None, None, None),
            P(("groups", "row"), "col", None),
            P(("groups", "row"), "col", None),
            P(("groups", "row"), "col"),
            P(("groups", "row", "col"), None),
        ),
        out_specs=(P(("groups", "row", "col"), None), P("groups", None), P("groups", None)),
        check_vma=False,
    )
```

```python
import functools
import math

import jax
import jax.numpy as jnp
from jax import lax
from jax.experimental import pallas as pl
from jax.experimental.pallas import tpu as pltpu
from jax.sharding import PartitionSpec as P

VMEM = pl.BlockSpec(memory_space=pltpu.VMEM)
HBM = pl.BlockSpec(memory_space=pltpu.HBM)


def dot(a, b, contract=((1,), (0,))):
    return lax.dot_general(a, b, (contract, ((), ())), preferred_element_type=jnp.float32)


def call(kernel, out_shape, in_specs, flops, name, *args):
    total = sum(a.size * a.dtype.itemsize for a in args)
    outs = out_shape if isinstance(out_shape, (tuple, list)) else (out_shape,)
    total += sum(math.prod(o.shape) * jnp.dtype(o.dtype).itemsize for o in outs)
    return pl.pallas_call(
        kernel,
        out_shape=out_shape,
        in_specs=in_specs,
        out_specs=jax.tree.map(lambda _: VMEM, out_shape),
        name=name,
        cost_estimate=pl.CostEstimate(flops=flops, bytes_accessed=total, transcendentals=0),
        compiler_params=pltpu.CompilerParams(vmem_limit_bytes=2 * total + (12 << 20)),
    )(*args)


def load(pairs, sems):
    copies = [pltpu.make_async_copy(*pair, sems.at[i]) for i, pair in enumerate(pairs)]
    for copy in copies:
        copy.start()
    return copies


def order_kernel(order_hbm, features_hbm, grads_hbm, out_ref, order_ref, features_ref, sems):
    nodes, feat = features_ref.shape
    pairs = (
        (order_hbm, order_ref), (features_hbm, features_ref), (grads_hbm, out_ref.at[:, feat:]),
    )
    for copy in load(pairs, sems):
        copy.wait()
    source = lax.broadcasted_iota(jnp.int32, (nodes, nodes), 0)
    picks = (source == order_ref[...]).astype(jnp.float32).astype(jnp.bfloat16)
    out_ref[:, :feat] = dot(picks, features_ref[...], ((0,), (0,))).astype(jnp.bfloat16)


def dense_kernel(
    blocks, count_ref, rows_hbm, cols_hbm, tiles_hbm, dense_ref, rows_ref, cols_ref, tiles_ref, sems
):
    copies = load(((rows_hbm, rows_ref), (cols_hbm, cols_ref), (tiles_hbm, tiles_ref)), sems)
    dense_ref[...] = jnp.zeros_like(dense_ref)
    for copy in copies:
        copy.wait()
    size = tiles_ref.shape[-1]
    own = lax.axis_index("row")

    def place(slot, carry):
        column = cols_ref[0, slot]
        piece = lax.bitwise_xor(column // blocks, own)
        row_at = pl.multiple_of(rows_ref[0, slot] * size, size)
        col_at = pl.multiple_of((piece * blocks + column % blocks) * size, size)
        dense_ref[pl.ds(row_at, size), pl.ds(col_at, size)] = tiles_ref[slot]
        return carry

    lax.fori_loop(0, count_ref[0, 0], place, 0)


def products(dense_ref, masks, pieces, chunk):
    depth = pieces[0].shape[0]
    for start in range(0, dense_ref.shape[0], chunk):
        total = None
        for k, piece in zip(masks, pieces):
            term = dot(dense_ref[start : start + chunk, k * depth : (k + 1) * depth], piece[...])
            total = term if total is None else total + term
        yield start, total


def early_kernel(masks, dense_ref, *refs):
    *pieces, out_ref = refs
    for start, total in products(dense_ref, masks, pieces, 128):
        out_ref[start : start + 128, :] = total


def first_kernel(masks, dense_ref, early_ref, *refs):
    *pieces, out_ref = refs
    for start, total in products(dense_ref, masks, pieces, 128):
        at = slice(start, start + 128)
        out_ref[at, :] = total + early_ref[at, :]


def middle_kernel(mine_ref, theirs_ref, first_ref, second_ref, projected_ref, out_ref):
    feat = first_ref.shape[0]
    half = first_ref.shape[1] // 2
    nodes = projected_ref.shape[0]
    col = lax.axis_index("col")
    hid_at = pl.ds(pl.multiple_of(col * half, half), half)
    summed = mine_ref[...] + theirs_ref[...]
    aggregated = summed[:, :feat].astype(jnp.bfloat16)
    back = summed[:, feat:].astype(jnp.bfloat16)
    first_half = first_ref[:, hid_at]
    second_half = second_ref[hid_at, :]

    at = pl.ds(pl.multiple_of(col * nodes, nodes), nodes)
    own = mine_ref[at, :feat] + theirs_ref[at, :feat]
    own_pre = dot(own.astype(jnp.bfloat16), first_ref[...])
    own_hidden = (own_pre * jax.nn.sigmoid(own_pre)).astype(jnp.bfloat16)
    projected_ref[...] = dot(own_hidden, second_ref[...]).astype(jnp.bfloat16)

    pre = dot(aggregated, first_half)
    gate = jax.nn.sigmoid(pre)
    hidden = (pre * gate).astype(jnp.bfloat16)
    hidden_grads = dot(back, second_half, ((1,), (1,)))
    pre_grads = (hidden_grads * gate * (1.0 + pre * (1.0 - gate))).astype(jnp.bfloat16)
    out_ref[:half, :] = dot(hidden, back, ((0,), (0,))).astype(jnp.bfloat16)
    out_ref[half:, :] = dot(aggregated, pre_grads, ((0,), (0,))).astype(jnp.bfloat16)


def early_logits_kernel(masks, dense_ref, *refs):
    *pieces, out_ref = refs
    nodes = out_ref.shape[0] // 2
    early_kernel(masks, dense_ref, *(piece.at[:nodes, :] for piece in pieces), out_ref)


def join_kernel(*refs):
    *parts, out_ref = refs
    nodes = parts[0].shape[0]
    for i, part in enumerate(parts):
        out_ref[i * nodes : (i + 1) * nodes, :] = part[...]


def sum_kernel(*refs):
    *parts, out_ref = refs
    at = slice(parts[0].shape[0] - out_ref.shape[0], None)
    total = parts[0][at, :].astype(jnp.float32)
    for part in parts[1:]:
        total = total + part[at, :].astype(jnp.float32)
    out_ref[...] = total.astype(jnp.bfloat16)


def second_kernel(masks, dense_ref, early_ref, *refs):
    *joined, keep_ref, send_ref = refs
    nodes = keep_ref.shape[0]
    pieces = [
        piece.at[start : start + nodes, :]
        for piece in joined for start in range(0, piece.shape[0], nodes)
    ]
    col = lax.axis_index("col")
    for where, ref in ((col, keep_ref), (1 - col, send_ref)):
        at = pl.ds(pl.multiple_of(where * nodes, nodes), nodes)
        early = early_ref.at[at, :]
        for start, total in products(dense_ref.at[at, :], masks, pieces, 128):
            ref[start : start + 128, :] = total + early[start : start + 128, :]


def last_kernel(scale, keep_ref, their_logits_ref, *refs):
    *parts, logits_ref, first_ref, second_ref = refs
    logits_ref[...] = (keep_ref[...] + their_logits_ref[...]).astype(jnp.bfloat16)
    half = second_ref.shape[0] // 2
    col = lax.axis_index("col")
    count = len(parts) // 2
    for where, some in ((col, parts[:count]), (1 - col, parts[count:])):
        total = some[0][...].astype(jnp.float32)
        for part in some[1:]:
            total = total + part[...].astype(jnp.float32)
        at = pl.ds(pl.multiple_of(where * half, half), half)
        second_ref[at, :] = total[:half, :] * scale
        first_ref[:, at] = total[half:, :] * scale


def exchange(x, axis, mask):
    size = lax.axis_size(axis)
    return lax.ppermute(x, axis, [(i, i ^ mask) for i in range(size)])


def near_size():
    return min(4, lax.axis_size("row"))


def from_far(x):
    size = lax.axis_size("row")
    return {mask: exchange(x, "row", mask) for mask in range(near_size(), size, near_size())}


def from_near(x, far):
    found = {low: exchange(x, "row", low) for low in range(1, near_size())}
    for mask, block in far.items():
        for low in range(1, near_size()):
            found[mask + low] = exchange(block, "row", low)
    return found


def arrival(near_order, last_order):
    size, near = lax.axis_size("row"), near_size()
    far = [*range(near, size, near)]
    first = [low for low in near_order if low < near]
    last = [mask + low for mask in far for low in last_order if low < near]
    return first, [*far, 0], last


def shards(
    features,
    node_order,
    weight_first,
    weight_second,
    adjacency_tiles,
    tile_rows,
    tile_cols,
    tile_counts,
    logit_grads,
):
    tiles = adjacency_tiles[0, 0]
    size = tiles.shape[-1]
    nodes, feat = features.shape
    hid, classes = weight_second.shape
    rows, cols = lax.axis_size("row"), lax.axis_size("col")
    slab = cols * nodes
    set_nodes = rows * nodes
    shape = jax.ShapeDtypeStruct
    bf16, f32 = jnp.bfloat16, jnp.float32

    slots = tiles.shape[0]
    in_hbm = functools.partial(pltpu.with_memory_space_constraint, memory_space=pltpu.HBM)
    source = pl.pallas_call(
        order_kernel,
        out_shape=shape((nodes, feat + classes), bf16),
        in_specs=[HBM] * 3,
        out_specs=VMEM,
        scratch_shapes=[
            pltpu.VMEM((1, nodes), jnp.int32),
            pltpu.VMEM((nodes, feat), bf16),
            pltpu.SemaphoreType.DMA((3,)),
        ],
        name="order",
        compiler_params=pltpu.CompilerParams(vmem_limit_bytes=8 << 20),
    )(in_hbm(node_order), in_hbm(features), in_hbm(logit_grads))
    dense = pl.pallas_call(
        functools.partial(dense_kernel, nodes // size),
        out_shape=shape((slab, set_nodes), bf16),
        in_specs=[pl.BlockSpec(memory_space=pltpu.SMEM)] + [HBM] * 3,
        out_specs=VMEM,
        scratch_shapes=[
            pltpu.SMEM((1, slots), jnp.int32),
            pltpu.SMEM((1, slots), jnp.int32),
            pltpu.VMEM(tiles.shape, bf16),
            pltpu.SemaphoreType.DMA((3,)),
        ],
        name="dense",
        cost_estimate=pl.CostEstimate(flops=1 * 10**6, bytes_accessed=4 * tiles.size, transcendentals=0),
        compiler_params=pltpu.CompilerParams(
            vmem_limit_bytes=4 * tiles.size + 4 * slab * set_nodes + (8 << 20)
        ),
    )(tile_counts, in_hbm(tile_rows[0]), in_hbm(tile_cols[0]), in_hbm(tiles))

    near, direct, late = arrival((3, 1, 2), (3, 1, 2))
    early = near + direct
    flops = 2 * slab * nodes * (feat + classes)
    far = from_far(source)
    found = {0: source} | far | from_near(source, far)
    partial = call(
        functools.partial(early_kernel, early), shape((slab, feat + classes), f32),
        [VMEM] * (1 + len(early)), 1 * 10**6, "early", dense, *(found[k] for k in early),
    )
    mine = call(
        functools.partial(first_kernel, late), shape((slab, feat + classes), f32),
        [VMEM] * (2 + len(late)), 40000 * 10**6, "first",
        dense, partial, *(found[k] for k in late),
    )
    projected, grads = call(
        middle_kernel, (shape((nodes, classes), bf16), shape((hid, classes), bf16)),
        [VMEM] * 4, 10 * slab * feat * hid,
        "middle", mine, exchange(mine, "col", 1), weight_first, weight_second,
    )
    flops = 2 * slab * nodes * classes
    far = from_far(projected)
    near_grads = from_near(grads, {})
    parts = [grads, *(near_grads[low] for low in (2, 3, 1))]
    total = call(
        sum_kernel, shape((hid, classes), bf16), [VMEM] * len(parts), 0, "sum", *parts
    )
    blocks = {0: projected} | far
    pair = call(
        join_kernel, shape((nodes * len(blocks), classes), bf16), [VMEM] * len(blocks), 15000000000,
        "join", *blocks.values(),
    )
    found = from_near(pair, {})
    partial = call(
        functools.partial(early_logits_kernel, [*blocks]), shape((slab, classes), f32),
        [VMEM] * (1 + len(blocks)), 15000000000, "early_logits", dense, *blocks.values(),
    )
    lows = [*(3, 2, 1)]
    keep, send = call(
        functools.partial(second_kernel, [k + low for low in lows for k in blocks]),
        (shape((nodes, classes), f32),) * 2,
        [VMEM] * (2 + len(lows)), 10**6, "second", dense, partial, *(found[k] for k in lows),
    )
    sums = [total, *from_far(total).values()]
    return call(
        functools.partial(last_kernel, 1.0 / math.sqrt(set_nodes * cols)),
        (shape((nodes, classes), bf16), shape((feat, hid), f32), shape((hid, classes), f32)),
        [VMEM] * (2 + 2 * len(sums)), 0, "last",
        keep, exchange(send, "col", 1), *sums, *(exchange(x, "col", 1) for x in sums),
    )


def solution(mesh):
    return jax.shard_map(
        shards,
        mesh=mesh,
        in_specs=(
            P(("groups", "row", "col"), None),
            P(("groups", "row", "col"), None),
            P(),
            P(),
            P(("groups", "row"), "col", None, None, None),
            P(("groups", "row"), "col", None),
            P(("groups", "row"), "col", None),
            P(("groups", "row"), "col"),
            P(("groups", "row", "col"), None),
        ),
        out_specs=(P(("groups", "row", "col"), None), P("groups", None), P("groups", None)),
        check_vma=False,
    )
```
